32 devices in a mesh: dp: 8 (over z, x), seq: 4 (over y, core).
Axes of the slice: x: 2, y: 2, z: 4, core: 2. Of those that a mesh axis runs over, the one named last changes fastest.
Arguments:
- tokens: bfloat16 [64, 512, 1024], P(('dp', 'seq')), may hold values from -6 to 6
- segments: int32 [64, 512], P(('dp', 'seq')), may hold values from 0 to 512, as said below
- cotangent: bfloat16 [64, 512, 1024], P(('dp', 'seq')), may hold values from -6 to 6
- w_qkv: bfloat16 [1024, 3072], P(('dp', 'seq')), may hold values from -0.1875 to 0.1875
- b_query: bfloat16 [1024], P(('dp', 'seq')), may hold values from -3 to 3
- b_value: bfloat16 [1024], P(('dp', 'seq')), may hold values from -3 to 3
- w_out: bfloat16 [1024, 1024], P(('dp', 'seq')), may hold values from -0.75 to 0.75
- b_out: bfloat16 [1024], P(('dp', 'seq')), may hold values from -3 to 3
- norm1_gain: bfloat16 [1024], P(('dp', 'seq')), may hold values from 0.5 to 1.5
- norm1_shift: bfloat16 [1024], P(('dp', 'seq')), may hold values from -3 to 3
- w_in: bfloat16 [1024, 4096], P(('dp', 'seq')), may hold values from -0.1875 to 0.1875
- b_in: bfloat16 [4096], P(('dp', 'seq')), may hold values from -3 to 3
- w_down: bfloat16 [4096, 1024], P(('dp', 'seq')), may hold values from -0.09375 to 0.09375
- b_down: bfloat16 [1024], P(('dp', 'seq')), may hold values from -3 to 3
- norm2_gain: bfloat16 [1024], P(('dp', 'seq')), may hold values from 0.5 to 1.5
- norm2_shift: bfloat16 [1024], P(('dp', 'seq')), may hold values from -3 to 3
Outputs:
- mixed: bfloat16 [64, 512, 1024], P(('dp', 'seq'))
- input_grad: float32 [64, 512, 1024], P(('dp', 'seq'))
- w_qkv_grad: float32 [1024, 3072], P(('dp', 'seq'))
- b_query_grad: float32 [1024], P(('dp', 'seq'))
- b_value_grad: float32 [1024], P(('dp', 'seq'))
- w_out_grad: float32 [1024, 1024], P(('dp', 'seq'))
- b_out_grad: float32 [1024], P(('dp', 'seq'))
- norm1_gain_grad: float32 [1024], P(('dp', 'seq'))
- norm1_shift_grad: float32 [1024], P(('dp', 'seq'))
- w_in_grad: float32 [1024, 4096], P(('dp', 'seq'))
- b_in_grad: float32 [4096], P(('dp', 'seq'))
- w_down_grad: float32 [4096, 1024], P(('dp', 'seq'))
- b_down_grad: float32 [1024], P(('dp', 'seq'))
- norm2_gain_grad: float32 [1024], P(('dp', 'seq'))
- norm2_shift_grad: float32 [1024], P(('dp', 'seq'))
The draws below stay inside these ranges and needn't reach their ends.
Inputs may be any that keep to these rules, and one draw needn't show every extreme that they name: `segments`: segment numbers never fall along a sequence and start at 0; the last document of every sequence has number 512.
All inputs are finite; a program needn't handle non-finite values.
Results may differ from the reference program's by a relative error of at most 0.013.
The reference program's roundings to bfloat16 on the way count: a program that leaves them out, or rounds other values in their place, can miss the bound.
Values may be sent and summed in bfloat16 or wider, within the bound.
A program may use at most 256 MiB of HBM per device.

```python
import jax
import jax.numpy as jnp
from jax import lax

D = 1024
FF = 4096
HEADS = 16
HEAD_DIM = 64
LENGTH = 512
SEQS = 64


def draw_segments(key, part):
    key = jax.random.fold_in(key, 7)
    key_start, key_end, key_marks = jax.random.split(key, 3)
    quarter = LENGTH // 4
    starts = jax.random.randint(key_start, (SEQS, 1), 1, quarter)
    ends = jax.random.randint(key_end, (SEQS, 1), LENGTH - quarter + 1, LENGTH)
    marks = (jax.random.randint(key_marks, (SEQS, LENGTH), 0, 48) == 0).astype(jnp.int32)
    places = jnp.arange(LENGTH, dtype=jnp.int32)[None, :]
    inside = (places > starts) & (places < ends)
    flags = jnp.where(inside, 0, marks)
    flags = jnp.where((places == starts) | (places == ends), 1, flags)
    flags = jnp.where(places == 0, 0, flags)
    counted = jnp.cumsum(flags, axis=1).astype(jnp.int32)
    last_doc = counted[:, -1:]
    return jnp.where(counted == last_doc, LENGTH, counted).astype(jnp.int32)


def with_spikes(entries, stream_key, source, target, parts, factor):
    def block_of(dim):
        return (jnp.arange(entries.shape[dim]) // (entries.shape[dim] // parts)).reshape((-1,) + (1,) * (entries.ndim - 1 - dim))

    first = jax.random.permutation(stream_key, parts)[block_of(target)]
    far = (block_of(target) + parts // 2) % parts
    return jnp.where((block_of(source) == first) | (block_of(source) == far), factor * entries, entries)


def levels(stream_key, extent, pieces, low, largest):
    def one(dim, blocks):
        steps = jax.random.uniform(jax.random.fold_in(jax.random.fold_in(stream_key, 6), dim), (blocks,), jnp.float32, low / len(pieces), largest / len(pieces))
        return jnp.repeat(jnp.exp(steps), extent[dim] // blocks).reshape((-1,) + (1,) * (len(extent) - dim - 1))

    level = one(*pieces[0])
    for cut in pieces[1:]:
        level = level * one(*cut)
    return level


def bell_draw(stream_key, shape, width, bound, pieces=(), kind=jnp.bfloat16):
    array = jax.random.normal(stream_key, shape, jnp.float32) * width
    if len(pieces) > 0:
        array = levels(stream_key, shape, pieces, -0.22, 0.18) * array
    return jnp.clip(array, min=-bound, max=bound).astype(kind)


def gaussian_with(stream_key, dims, width, reach, cuts, heavy, kind=jnp.bfloat16):
    array = width * jax.random.normal(stream_key, dims, jnp.float32)
    if cuts:
        array = array * levels(stream_key, dims, cuts, -0.22, 0.18)
    return jnp.clip(with_spikes(array, jax.random.fold_in(stream_key, 3), *heavy), -reach, reach).astype(kind)


def setup_inputs(seed: int = 0) -> dict:
    key_list = jax.random.split(jax.random.key(seed), 17)
    return {
        "tokens": gaussian_with(key_list[0], (SEQS, LENGTH, D), 1.0, 6.0, ((0, 32),), (0, 2, 32, 2.75)),
        "segments": draw_segments(jax.random.fold_in(key_list[16], 71), 0),
        "cotangent": gaussian_with(key_list[2], (SEQS, LENGTH, D), 1.0, 6.0, ((0, 32),), (0, 2, 32, 2.75)),
        "w_qkv": bell_draw(key_list[3], (D, 3 * D), D ** -0.5, 0.1875, ((0, 32),)),
        "b_query": bell_draw(key_list[4], (D,), 0.5, 3.0, ((0, 32),)),
        "b_value": bell_draw(key_list[5], (D,), 0.5, 3.0, ((0, 32),)),
        "w_out": bell_draw(key_list[6], (D, D), (D // 16) ** -0.5, 0.75, ((0, 32),)),
        "b_out": bell_draw(key_list[7], (D,), 0.5, 3.0, ((0, 32),)),
        "norm1_gain": jnp.clip(1.0 + 0.1 * jax.random.normal(key_list[8], (D,), jnp.float32), 0.5, 1.5).astype(jnp.bfloat16),
        "norm1_shift": bell_draw(key_list[9], (D,), 0.5, 3.0, ((0, 32),)),
        "w_in": bell_draw(key_list[10], (D, FF), D ** -0.5, 0.1875, ((0, 32),)),
        "b_in": bell_draw(key_list[11], (FF,), 0.5, 3.0, ((0, 32),)),
        "w_down": bell_draw(key_list[12], (FF, D), FF ** -0.5, 0.09375, ((0, 32),)),
        "b_down": bell_draw(key_list[13], (D,), 0.5, 3.0, ((0, 32),)),
        "norm2_gain": jnp.clip(1.0 + 0.1 * jax.random.normal(key_list[14], (D,), jnp.float32), 0.5, 1.5).astype(jnp.bfloat16),
        "norm2_shift": bell_draw(key_list[15], (D,), 0.5, 3.0, ((0, 32),)),
    }


eps_norm = 1e-05
highest = lax.Precision.HIGHEST

@jax.custom_vjp
def low(v):
    return lax.optimization_barrier(v.astype(jnp.bfloat16)).astype(jnp.float32)

@jax.custom_vjp
def low_back(v):
    return v

def low_keep(v):
    return (low(v), None)

def low_pass(kept, grad):
    return (grad,)

def back_keep(v):
    return (v, None)

def back_low(kept, grad):
    return (low(grad),)
low.defvjp(low_keep, low_pass)
low_back.defvjp(back_keep, back_low)

def matmul(left, right):
    return jnp.dot(left, right, precision=highest, preferred_element_type=jnp.float32)

def layer_norm(hidden, gain, shift):
    center = hidden - lax.optimization_barrier(jnp.mean(hidden, axis=-1, keepdims=True))
    spread = lax.optimization_barrier(jnp.mean(center * center, axis=-1, keepdims=True))
    return center * lax.rsqrt(spread + eps_norm) * gain + shift

def attend_block(query_heads, key_heads, value_heads, seg_ids):
    scores = jnp.einsum('qhe,khe->hqk', query_heads, key_heads, precision=highest) * HEAD_DIM ** (-0.5)
    scores = low_back(scores)
    same_doc = seg_ids[:, None] == seg_ids[None, :]
    scores = jnp.where(same_doc[None], scores, -1e+30)
    row_peak = lax.optimization_barrier(jnp.max(scores, axis=-1, keepdims=True))
    exp_scores = jnp.exp(scores - row_peak)
    soft_probs = exp_scores / lax.optimization_barrier(jnp.sum(exp_scores, axis=-1, keepdims=True))
    return jnp.einsum('hqk,khe->qhe', low(soft_probs), value_heads, precision=highest)

def sequence_forward(params, inputs, seg_ids):
    w_qkv, b_query, b_value, w_out, b_out, gain_one, shift_one, w_in, b_in, w_down, b_down, gain_two, shift_two = params
    model_width = HEADS * HEAD_DIM
    qkv_bias = jnp.concatenate([b_query, jnp.zeros_like(b_query), b_value])
    qkv = low_back(low(matmul(inputs, w_qkv) + qkv_bias))
    query_heads = qkv[:, :model_width].reshape(LENGTH, HEADS, HEAD_DIM)
    key_heads = qkv[:, model_width:2 * model_width].reshape(LENGTH, HEADS, HEAD_DIM)
    value_heads = qkv[:, 2 * model_width:].reshape(LENGTH, HEADS, HEAD_DIM)
    blocks = jax.checkpoint(attend_block)(query_heads, key_heads, value_heads, seg_ids)
    attended = low_back(low(blocks.reshape(LENGTH, model_width)))
    hidden_one = inputs + low_back(matmul(attended, w_out) + b_out)
    normed_one = layer_norm(hidden_one, gain_one, shift_one)
    pre_gelu = low_back(matmul(low(normed_one), w_in) + b_in)
    activated = low(jax.nn.gelu(pre_gelu, approximate=False))
    hidden_two = normed_one + low_back(matmul(activated, w_down) + b_down)
    return layer_norm(hidden_two, gain_two, shift_two)

def reference(tokens, segments, cotangent, w_qkv, b_query, b_value, w_out, b_out, norm1_gain, norm1_shift, w_in, b_in, w_down, b_down, norm2_gain, norm2_shift):
    params = tuple((param.astype(jnp.float32) for param in (w_qkv, b_query, b_value, w_out, b_out, norm1_gain, norm1_shift, w_in, b_in, w_down, b_down, norm2_gain, norm2_shift)))

    def one_sequence(summed, item):
        seq_tokens, seq_ids, seq_cot = item
        result, pull = jax.vjp(lambda par, inp: sequence_forward(par, inp, seq_ids), params, seq_tokens.astype(jnp.float32))
        param_grads, token_grad = pull(seq_cot.astype(jnp.float32))
        summed = jax.tree.map(jnp.add, summed, param_grads)
        return (summed, (result.astype(jnp.bfloat16), token_grad))
    zeros_start = jax.tree.map(jnp.zeros_like, params)
    grads, (mixed, input_grad) = lax.scan(one_sequence, zeros_start, (tokens, segments, cotangent))
    return (mixed, input_grad, grads[0], grads[1], grads[2], grads[3], grads[4], grads[5], grads[6], grads[7], grads[8], grads[9], grads[10], grads[11], grads[12])
```

```python
import jax
import jax.numpy as jnp
from jax import lax
from jax.experimental import pallas as pl
from jax.experimental.pallas import tpu as pltpu
from jax.sharding import PartitionSpec as P

HEADS = 16
HEAD_DIM = 64


eps_norm = 1e-05


def layer_norm(hidden, gain, shift):
    center = hidden - jnp.mean(hidden, axis=-1, keepdims=True)
    spread = jnp.mean(center * center, axis=-1, keepdims=True)
    return center * lax.rsqrt(spread + eps_norm) * gain + shift


def gelu_exact(pre_gelu):
    return jax.nn.gelu(pre_gelu, approximate=False)


def product(left, right):
    return jnp.dot(left, right, preferred_element_type=jnp.float32)


def left_major(left, right):
    return lax.dot_general(
        left, right, (((0,), (0,)), ((), ())), preferred_element_type=jnp.float32
    )


def right_major(left, right):
    return lax.dot_general(
        left, right, (((1,), (1,)), ((), ())), preferred_element_type=jnp.float32
    )


def column_sums(matrix):
    return jnp.sum(matrix.astype(jnp.float32), axis=0)


SCALE = HEAD_DIM ** (-0.5)
PAIR = 2 * HEAD_DIM


def head_mask(length, head):
    lanes = lax.broadcasted_iota(jnp.int32, (length, PAIR), 1)
    return (lanes >= head * HEAD_DIM) & (lanes < (head + 1) * HEAD_DIM)


def keep_head(block, mask):
    return jnp.where(mask, block, jnp.zeros_like(block))


def head_probs(query, key, same_doc):
    scores = jnp.where(same_doc, right_major(query, key) * SCALE, -1e30)
    exp_scores = jnp.exp(scores - jnp.max(scores, axis=-1, keepdims=True))
    return exp_scores * (1.0 / jnp.sum(exp_scores, axis=-1, keepdims=True))


def attend_kernel(seg_col, seg_row, query_ref, key_ref, value_ref, out_ref):
    same_doc = seg_col[0] == seg_row[0]
    query, key, value = query_ref[...], key_ref[...], value_ref[...]
    total = jnp.zeros(query.shape, jnp.float32)
    for head in range(2):
        mask = head_mask(query.shape[0], head)
        probs = head_probs(keep_head(query, mask), key, same_doc)
        total += product(probs.astype(jnp.bfloat16), keep_head(value, mask))
    out_ref[...] = total.astype(jnp.bfloat16)


def attend_back_kernel(seg_col, seg_row, query_ref, key_ref, value_ref, grad_ref, out_ref):
    same_doc = seg_col[0] == seg_row[0]
    query, key, value, grad = query_ref[...], key_ref[...], value_ref[...], grad_ref[...]
    query_grad = jnp.zeros(query.shape, jnp.float32)
    key_grad = jnp.zeros(query.shape, jnp.float32)
    value_grad = jnp.zeros(query.shape, jnp.float32)
    for head in range(2):
        mask = head_mask(query.shape[0], head)
        query_own, grad_own = keep_head(query, mask), keep_head(grad, mask)
        probs = head_probs(query_own, key, same_doc)
        prob_grad = right_major(grad_own, value)
        inner_sum = jnp.sum(probs * prob_grad, axis=-1, keepdims=True)
        score_low = (probs * (prob_grad - inner_sum)).astype(jnp.bfloat16)
        query_grad += product(score_low, keep_head(key, mask))
        key_grad += left_major(score_low, query_own)
        value_grad += left_major(probs.astype(jnp.bfloat16), grad_own)
    out_ref[0] = (query_grad * SCALE).astype(jnp.bfloat16)
    out_ref[1] = (key_grad * SCALE).astype(jnp.bfloat16)
    out_ref[2] = value_grad.astype(jnp.bfloat16)


def attention_specs(seq_len, pairs):
    def column_block(first):
        return pl.BlockSpec((seq_len, PAIR), lambda seq, pair: (seq, first + pair))

    return [
        pl.BlockSpec((1, seq_len, 1), lambda seq, pair: (seq, 0, 0)),
        pl.BlockSpec((1, 1, seq_len), lambda seq, pair: (seq, 0, 0)),
        column_block(0),
        column_block(pairs),
        column_block(2 * pairs),
        column_block(0),
    ]


def attend(segments, qkv):
    seq_count, seq_len = segments.shape
    pairs = HEADS // 2
    specs = attention_specs(seq_len, pairs)
    area = seq_count * HEADS * seq_len * seq_len
    return pl.pallas_call(
        attend_kernel,
        grid=(seq_count, pairs),
        in_specs=specs[:5],
        out_specs=specs[5],
        out_shape=jax.ShapeDtypeStruct((qkv.shape[0], HEADS * HEAD_DIM), jnp.bfloat16),
        compiler_params=pltpu.CompilerParams(vmem_limit_bytes=40 * 2**20),
        cost_estimate=pl.CostEstimate(
            flops=4 * PAIR * area, bytes_accessed=8 * qkv.size // 3, transcendentals=area
        ),
    )(segments[:, :, None], segments[:, None, :], qkv, qkv, qkv)


def attend_back(segments, qkv, attended_grad):
    seq_count, seq_len = segments.shape
    pairs = HEADS // 2
    specs = attention_specs(seq_len, pairs)
    area = seq_count * HEADS * seq_len * seq_len
    return pl.pallas_call(
        attend_back_kernel,
        grid=(seq_count, pairs),
        in_specs=specs,
        out_specs=pl.BlockSpec((3, seq_len, PAIR), lambda seq, pair: (0, seq, pair)),
        out_shape=jax.ShapeDtypeStruct((3, qkv.shape[0], HEADS * HEAD_DIM), jnp.bfloat16),
        compiler_params=pltpu.CompilerParams(vmem_limit_bytes=40 * 2**20),
        cost_estimate=pl.CostEstimate(
            flops=10 * PAIR * area, bytes_accessed=14 * qkv.size // 3, transcendentals=area
        ),
    )(segments[:, :, None], segments[:, None, :], qkv, qkv, qkv, attended_grad)


def scatter_rows(grad, swap):
    dp_size, seq_size = lax.axis_size("dp"), lax.axis_size("seq")
    dp_bits, seq_bits = dp_size.bit_length() - 1, seq_size.bit_length() - 1
    near = [("dp", 0)] + [("seq", bit) for bit in range(1, seq_bits)]
    if swap:
        near = near[::-1]
    order = [("seq", 0)] + near + [("dp", bit) for bit in range(dp_bits - 1, 0, -1)]
    width = grad.shape[1]
    left = [("dp", bit) for bit in range(dp_bits - 1, -1, -1)]
    left += [("seq", bit) for bit in range(seq_bits - 1, -1, -1)]
    part = grad.astype(jnp.bfloat16)
    for name, bit in order:
        place = left.index((name, bit))
        outer = 2**place
        left.remove((name, bit))
        view = part.reshape(outer, 2, -1, width)
        mine = (lax.axis_index(name) >> bit) & 1
        size = lax.axis_size(name)
        send = lax.dynamic_index_in_dim(view, 1 - mine, 1, keepdims=False)
        keep = lax.dynamic_index_in_dim(view, mine, 1, keepdims=False)
        came = lax.ppermute(send, name, [(i, i ^ (1 << bit)) for i in range(size)])
        total = keep.astype(jnp.float32) + came.astype(jnp.float32)
        part = total.astype(jnp.bfloat16) if left else total
    return part.reshape(-1, width)


def shards(
    tokens,
    segments,
    cotangent,
    w_qkv,
    b_query,
    b_value,
    w_out,
    b_out,
    norm1_gain,
    norm1_shift,
    w_in,
    b_in,
    w_down,
    b_down,
    norm2_gain,
    norm2_shift,
):
    rows = w_qkv.shape[0]
    vectors = (b_query, b_value, b_out, norm1_gain, norm1_shift, b_down, norm2_gain, norm2_shift)
    small = jnp.concatenate(
        [vector[:, None] for vector in vectors] + [b_in.reshape(rows, -1)], axis=1
    )
    small = jnp.pad(small, ((0, 0), (0, 128 - small.shape[1])))
    first = lax.all_gather(
        jnp.concatenate([w_qkv, small], axis=1), ("dp", "seq"), axis=0, tiled=True
    )
    full_out = lax.all_gather(w_out, ("dp", "seq"), axis=0, tiled=True)
    full_in = lax.all_gather(w_in, ("dp", "seq"), axis=0, tiled=True)
    full_down = lax.all_gather(w_down, ("dp", "seq"), axis=0, tiled=True)
    full_qkv = first[:, : w_qkv.shape[1]]
    small_full = first[:, w_qkv.shape[1] :]
    by_row = small_full[:, : len(vectors)].T
    (
        full_bquery,
        full_bvalue,
        full_bout,
        full_gain_one,
        full_shift_one,
        full_bdown,
        full_gain_two,
        full_shift_two,
    ) = [by_row[i] for i in range(len(vectors))]
    full_bin = small_full[:, len(vectors) : len(vectors) + b_in.shape[0] // rows].reshape(-1)
    model_width = HEADS * HEAD_DIM
    seq_count = tokens.shape[0]
    seq_len = tokens.shape[1]
    tok_rows = seq_count * seq_len
    inputs = tokens.reshape(tok_rows, model_width)
    qkv_bias = jnp.concatenate([full_bquery, jnp.zeros_like(full_bquery), full_bvalue]).astype(
        jnp.float32
    )
    qkv = (product(inputs, full_qkv) + qkv_bias).astype(jnp.bfloat16)
    attended = attend(segments, qkv)
    hidden_one = (
        inputs.astype(jnp.float32) + product(attended, full_out) + full_bout.astype(jnp.float32)
    )
    normed_one, norm_one_pull = jax.vjp(
        layer_norm,
        hidden_one,
        full_gain_one.astype(jnp.float32),
        full_shift_one.astype(jnp.float32),
    )
    normed_low = normed_one.astype(jnp.bfloat16)
    pre_gelu = product(normed_low, full_in) + full_bin.astype(jnp.float32)
    activated, gelu_pull = jax.vjp(gelu_exact, pre_gelu)
    act_low = activated.astype(jnp.bfloat16)
    hidden_two = normed_one + product(act_low, full_down) + full_bdown.astype(jnp.float32)
    mixed_full, norm_two_pull = jax.vjp(
        layer_norm,
        hidden_two,
        full_gain_two.astype(jnp.float32),
        full_shift_two.astype(jnp.float32),
    )
    mixed = mixed_full.astype(jnp.bfloat16).reshape(seq_count, seq_len, model_width)
    upstream = cotangent.reshape(tok_rows, model_width).astype(jnp.float32)
    grad_two, gain_two_grad, shift_two_grad = norm_two_pull(upstream)
    grad_two_low = grad_two.astype(jnp.bfloat16)
    down_grad = left_major(act_low, grad_two_low)
    down_bias_grad = column_sums(grad_two_low)
    (pre_grad,) = gelu_pull(right_major(grad_two_low, full_down))
    pre_low = pre_grad.astype(jnp.bfloat16)
    in_grad = left_major(normed_low, pre_low)
    in_bias_grad = column_sums(pre_low)
    normed_grad = right_major(pre_low, full_in) + grad_two
    grad_one, gain_one_grad, shift_one_grad = norm_one_pull(normed_grad)
    grad_one_low = grad_one.astype(jnp.bfloat16)
    out_grad = left_major(attended, grad_one_low)
    out_bias_grad = column_sums(grad_one_low)
    attended_grad = right_major(grad_one_low, full_out).astype(jnp.bfloat16)
    three = attend_back(segments, qkv, attended_grad)
    qkv_grad = jnp.concatenate([three[0], three[1], three[2]], axis=1)
    qkv_weight_grad = left_major(inputs, qkv_grad)
    qkv_sums = column_sums(qkv_grad)
    input_grad = (right_major(qkv_grad, full_qkv) + grad_one).reshape(
        seq_count, seq_len, model_width
    )
    sums = (
        qkv_sums[:model_width],
        qkv_sums[2 * model_width :],
        out_bias_grad,
        gain_one_grad,
        shift_one_grad,
        down_bias_grad,
        gain_two_grad,
        shift_two_grad,
    )
    small_grad = jnp.concatenate(
        [jnp.stack(sums), in_bias_grad.reshape(model_width, -1).T], axis=0
    )
    small_grad = jnp.pad(small_grad, ((0, 128 - small_grad.shape[0]), (0, 0))).T
    down_shard = scatter_rows(down_grad, False)
    in_shard = scatter_rows(in_grad, True)
    out_shard = scatter_rows(out_grad, False)
    half = qkv_weight_grad.shape[1] // 2
    qkv_shard = jnp.concatenate(
        [
            scatter_rows(qkv_weight_grad[:, :half], True),
            scatter_rows(qkv_weight_grad[:, half:], False),
        ],
        axis=1,
    )
    small_shard = scatter_rows(small_grad, True)
    columns = [small_shard[:, i] for i in range(len(vectors))]
    (
        bquery_shard,
        bvalue_shard,
        out_bias_shard,
        gain_one_shard,
        shift_one_shard,
        down_bias_shard,
        gain_two_shard,
        shift_two_shard,
    ) = columns
    in_bias_shard = small_shard[:, len(vectors) : len(vectors) + b_in.shape[0] // rows].reshape(-1)
    return (
        mixed,
        input_grad,
        qkv_shard,
        bquery_shard,
        bvalue_shard,
        out_shard,
        out_bias_shard,
        gain_one_shard,
        shift_one_shard,
        in_shard,
        in_bias_shard,
        down_shard,
        down_bias_shard,
        gain_two_shard,
        shift_two_shard,
    )


def solution(mesh):
    in_specs = (
        P(("dp", "seq"), None, None),
        P(("dp", "seq"), None),
        P(("dp", "seq"), None, None),
        P(("dp", "seq"), None),
        P(("dp", "seq")),
        P(("dp", "seq")),
        P(("dp", "seq"), None),
        P(("dp", "seq")),
        P(("dp", "seq")),
        P(("dp", "seq")),
        P(("dp", "seq"), None),
        P(("dp", "seq")),
        P(("dp", "seq"), None),
        P(("dp", "seq")),
        P(("dp", "seq")),
        P(("dp", "seq")),
    )
    out_specs = (
        P(("dp", "seq"), None, None),
        P(("dp", "seq"), None, None),
        P(("dp", "seq"), None),
        P(("dp", "seq")),
        P(("dp", "seq")),
        P(("dp", "seq"), None),
        P(("dp", "seq")),
        P(("dp", "seq")),
        P(("dp", "seq")),
        P(("dp", "seq"), None),
        P(("dp", "seq")),
        P(("dp", "seq"), None),
        P(("dp", "seq")),
        P(("dp", "seq")),
        P(("dp", "seq")),
    )
    return jax.shard_map(shards, mesh=mesh, in_specs=in_specs, out_specs=out_specs, check_vma=False)
```

```python
import jax
import jax.numpy as jnp
from jax import lax
from jax.experimental import pallas as pl
from jax.experimental.pallas import tpu as pltpu
from jax.sharding import PartitionSpec as P

HEADS = 16
HEAD_DIM = 64


eps_norm = 1e-05


def layer_norm(hidden, gain, shift):
    center = hidden - jnp.mean(hidden, axis=-1, keepdims=True)
    spread = jnp.mean(center * center, axis=-1, keepdims=True)
    return center * lax.rsqrt(spread + eps_norm) * gain + shift


def gelu_exact(pre_gelu):
    return jax.nn.gelu(pre_gelu, approximate=False)


def product(left, right):
    return jnp.dot(left, right, preferred_element_type=jnp.float32)


def left_major(left, right):
    return lax.dot_general(
        left, right, (((0,), (0,)), ((), ())), preferred_element_type=jnp.float32
    )


def right_major(left, right):
    return lax.dot_general(
        left, right, (((1,), (1,)), ((), ())), preferred_element_type=jnp.float32
    )


def column_sums(matrix):
    return jnp.sum(matrix.astype(jnp.float32), axis=0)


SCALE = HEAD_DIM ** (-0.5)
PAIR = 2 * HEAD_DIM


def head_mask(length, head):
    lanes = lax.broadcasted_iota(jnp.int32, (length, PAIR), 1)
    return (lanes >= head * HEAD_DIM) & (lanes < (head + 1) * HEAD_DIM)


def keep_head(block, mask):
    return jnp.where(mask, block, jnp.zeros_like(block))


def head_probs(query, key, same_doc):
    scores = jnp.where(same_doc, right_major(query, key) * SCALE, -1e30)
    exp_scores = jnp.exp(scores - jnp.max(scores, axis=-1, keepdims=True))
    return exp_scores * (1.0 / jnp.sum(exp_scores, axis=-1, keepdims=True))


def attend_kernel(seg_col, seg_row, query_ref, key_ref, value_ref, out_ref):
    same_doc = seg_col[0] == seg_row[0]
    query, key, value = query_ref[...], key_ref[...], value_ref[...]
    total = jnp.zeros(query.shape, jnp.float32)
    for head in range(2):
        mask = head_mask(query.shape[0], head)
        probs = head_probs(keep_head(query, mask), key, same_doc)
        total += product(probs.astype(jnp.bfloat16), keep_head(value, mask))
    out_ref[...] = total.astype(jnp.bfloat16)


def attend_back_kernel(seg_col, seg_row, query_ref, key_ref, value_ref, grad_ref, out_ref):
    same_doc = seg_col[0] == seg_row[0]
    query, key, value, grad = query_ref[...], key_ref[...], value_ref[...], grad_ref[...]
    query_grad = jnp.zeros(query.shape, jnp.float32)
    key_grad = jnp.zeros(query.shape, jnp.float32)
    value_grad = jnp.zeros(query.shape, jnp.float32)
    for head in range(2):
        mask = head_mask(query.shape[0], head)
        query_own, grad_own = keep_head(query, mask), keep_head(grad, mask)
        probs = head_probs(query_own, key, same_doc)
        prob_grad = right_major(grad_own, value)
        inner_sum = jnp.sum(probs * prob_grad, axis=-1, keepdims=True)
        score_low = (probs * (prob_grad - inner_sum)).astype(jnp.bfloat16)
        query_grad += product(score_low, keep_head(key, mask))
        key_grad += left_major(score_low, query_own)
        value_grad += left_major(probs.astype(jnp.bfloat16), grad_own)
    out_ref[0] = (query_grad * SCALE).astype(jnp.bfloat16)
    out_ref[1] = (key_grad * SCALE).astype(jnp.bfloat16)
    out_ref[2] = value_grad.astype(jnp.bfloat16)


def attention_specs(seq_len, pairs):
    def column_block(first):
        return pl.BlockSpec((seq_len, PAIR), lambda seq, pair: (seq, first + pair))

    return [
        pl.BlockSpec((1, seq_len, 1), lambda seq, pair: (seq, 0, 0)),
        pl.BlockSpec((1, 1, seq_len), lambda seq, pair: (seq, 0, 0)),
        column_block(0),
        column_block(pairs),
        column_block(2 * pairs),
        column_block(0),
    ]


def attend(segments, qkv):
    seq_count, seq_len = segments.shape
    pairs = HEADS // 2
    specs = attention_specs(seq_len, pairs)
    area = seq_count * HEADS * seq_len * seq_len
    return pl.pallas_call(
        attend_kernel,
        grid=(seq_count, pairs),
        in_specs=specs[:5],
        out_specs=specs[5],
        out_shape=jax.ShapeDtypeStruct((qkv.shape[0], HEADS * HEAD_DIM), jnp.bfloat16),
        compiler_params=pltpu.CompilerParams(vmem_limit_bytes=40 * 2**20),
        cost_estimate=pl.CostEstimate(
            flops=4 * PAIR * area, bytes_accessed=8 * qkv.size // 3, transcendentals=area
        ),
    )(segments[:, :, None], segments[:, None, :], qkv, qkv, qkv)


def attend_back(segments, qkv, attended_grad):
    seq_count, seq_len = segments.shape
    pairs = HEADS // 2
    specs = attention_specs(seq_len, pairs)
    area = seq_count * HEADS * seq_len * seq_len
    return pl.pallas_call(
        attend_back_kernel,
        grid=(seq_count, pairs),
        in_specs=specs,
        out_specs=pl.BlockSpec((3, seq_len, PAIR), lambda seq, pair: (0, seq, pair)),
        out_shape=jax.ShapeDtypeStruct((3, qkv.shape[0], HEADS * HEAD_DIM), jnp.bfloat16),
        compiler_params=pltpu.CompilerParams(vmem_limit_bytes=40 * 2**20),
        cost_estimate=pl.CostEstimate(
            flops=10 * PAIR * area, bytes_accessed=14 * qkv.size // 3, transcendentals=area
        ),
    )(segments[:, :, None], segments[:, None, :], qkv, qkv, qkv, attended_grad)


def scatter_start(grad, swap):
    dp_size, seq_size = lax.axis_size("dp"), lax.axis_size("seq")
    dp_bits, seq_bits = dp_size.bit_length() - 1, seq_size.bit_length() - 1
    near = [("dp", 0)] + [("seq", bit) for bit in range(1, seq_bits)]
    if swap:
        near = near[::-1]
    order = [("seq", 0)] + near + [("dp", bit) for bit in range(dp_bits - 1, 0, -1)]
    left = [("dp", bit) for bit in range(dp_bits - 1, -1, -1)]
    left += [("seq", bit) for bit in range(seq_bits - 1, -1, -1)]
    return grad.astype(jnp.bfloat16), left, order


def scatter_steps(state, steps):
    part, left, order = state
    left = list(left)
    width = part.shape[-1]
    for name, bit in order[:steps]:
        place = left.index((name, bit))
        left.remove((name, bit))
        view = part.reshape(2**place, 2, -1, width)
        mine = (lax.axis_index(name) >> bit) & 1
        size = lax.axis_size(name)
        send = lax.dynamic_index_in_dim(view, 1 - mine, 1, keepdims=False)
        keep = lax.dynamic_index_in_dim(view, mine, 1, keepdims=False)
        came = lax.ppermute(send, name, [(i, i ^ (1 << bit)) for i in range(size)])
        total = keep.astype(jnp.float32) + came.astype(jnp.float32)
        part = total.astype(jnp.bfloat16) if left else total
    return part, left, order[steps:]


def scatter_end(state):
    part = scatter_steps(state, len(state[2]))[0]
    return part.reshape(-1, part.shape[-1])


def tie(values, states):
    values, parts = lax.optimization_barrier((values, [state[0] for state in states]))
    return values, [(part,) + state[1:] for part, state in zip(parts, states)]


def shards(
    tokens,
    segments,
    cotangent,
    w_qkv,
    b_query,
    b_value,
    w_out,
    b_out,
    norm1_gain,
    norm1_shift,
    w_in,
    b_in,
    w_down,
    b_down,
    norm2_gain,
    norm2_shift,
):
    rows = w_qkv.shape[0]
    vectors = (b_query, b_value, b_out, norm1_gain, norm1_shift, b_down, norm2_gain, norm2_shift)
    small = jnp.concatenate(
        [vector[:, None] for vector in vectors] + [b_in.reshape(rows, -1)], axis=1
    )
    small = jnp.pad(small, ((0, 0), (0, 128 - small.shape[1])))
    first = lax.all_gather(
        jnp.concatenate([w_qkv, w_out, small], axis=1), ("dp", "seq"), axis=0, tiled=True
    )
    full_in = lax.all_gather(w_in, ("dp", "seq"), axis=0, tiled=True)
    full_down = lax.all_gather(w_down, ("dp", "seq"), axis=0, tiled=True)
    full_qkv = first[:, : w_qkv.shape[1]]
    full_out = first[:, w_qkv.shape[1] : w_qkv.shape[1] + w_out.shape[1]]
    small_full = first[:, w_qkv.shape[1] + w_out.shape[1] :]
    by_row = small_full[:, : len(vectors)].T
    (
        full_bquery,
        full_bvalue,
        full_bout,
        full_gain_one,
        full_shift_one,
        full_bdown,
        full_gain_two,
        full_shift_two,
    ) = [by_row[i] for i in range(len(vectors))]
    full_bin = small_full[:, len(vectors) : len(vectors) + b_in.shape[0] // rows].reshape(-1)
    model_width = HEADS * HEAD_DIM
    seq_count = tokens.shape[0]
    seq_len = tokens.shape[1]
    tok_rows = seq_count * seq_len
    inputs = tokens.reshape(tok_rows, model_width)
    qkv_bias = jnp.concatenate([full_bquery, jnp.zeros_like(full_bquery), full_bvalue]).astype(
        jnp.float32
    )
    qkv = (product(inputs, full_qkv) + qkv_bias).astype(jnp.bfloat16)
    attended = attend(segments, qkv)
    hidden_one = (
        inputs.astype(jnp.float32) + product(attended, full_out) + full_bout.astype(jnp.float32)
    )
    normed_one, norm_one_pull = jax.vjp(
        layer_norm,
        hidden_one,
        full_gain_one.astype(jnp.float32),
        full_shift_one.astype(jnp.float32),
    )
    normed_low = normed_one.astype(jnp.bfloat16)
    pre_gelu = product(normed_low, full_in) + full_bin.astype(jnp.float32)
    activated, gelu_pull = jax.vjp(gelu_exact, pre_gelu)
    act_low = activated.astype(jnp.bfloat16)
    hidden_two = normed_one + product(act_low, full_down) + full_bdown.astype(jnp.float32)
    mixed_full, norm_two_pull = jax.vjp(
        layer_norm,
        hidden_two,
        full_gain_two.astype(jnp.float32),
        full_shift_two.astype(jnp.float32),
    )
    mixed = mixed_full.astype(jnp.bfloat16).reshape(seq_count, seq_len, model_width)
    upstream = cotangent.reshape(tok_rows, model_width).astype(jnp.float32)
    grad_two, gain_two_grad, shift_two_grad = norm_two_pull(upstream)
    grad_two_low = grad_two.astype(jnp.bfloat16)
    down_grad = left_major(act_low, grad_two_low)
    down_bias_grad = column_sums(grad_two_low)
    (grad_two_low,), (down,) = tie((grad_two_low,), [scatter_start(down_grad, False)])
    (pre_grad,) = gelu_pull(right_major(grad_two_low, full_down))
    pre_low = pre_grad.astype(jnp.bfloat16)
    in_bias_grad = column_sums(pre_low)
    (pre_low,), (down,) = tie((pre_low,), [scatter_steps(down, 1)])
    in_grad = left_major(normed_low, pre_low)
    normed_grad = right_major(pre_low, full_in) + grad_two
    (normed_grad,), (down, inward) = tie(
        (normed_grad,), [scatter_steps(down, 1), scatter_start(in_grad, True)]
    )
    grad_one, gain_one_grad, shift_one_grad = norm_one_pull(normed_grad)
    grad_one_low = grad_one.astype(jnp.bfloat16)
    out_grad = left_major(attended, grad_one_low)
    out_bias_grad = column_sums(grad_one_low)
    attended_grad = right_major(grad_one_low, full_out).astype(jnp.bfloat16)
    (attended_grad,), (inward, outward) = tie(
        (attended_grad,), [scatter_steps(inward, 1), scatter_start(out_grad, False)]
    )
    three = attend_back(segments, qkv, attended_grad)
    (three,), (down, inward, outward) = tie(
        (three,), [scatter_steps(down, 2), scatter_steps(inward, 1), scatter_steps(outward, 1)]
    )
    qkv_grad = jnp.concatenate([three[0], three[1], three[2]], axis=1)
    qkv_weight_grad = left_major(inputs, qkv_grad)
    qkv_sums = column_sums(qkv_grad)
    input_grad = (right_major(qkv_grad, full_qkv) + grad_one).reshape(
        seq_count, seq_len, model_width
    )
    sums = (
        qkv_sums[:model_width],
        qkv_sums[2 * model_width :],
        out_bias_grad,
        gain_one_grad,
        shift_one_grad,
        down_bias_grad,
        gain_two_grad,
        shift_two_grad,
    )
    small_grad = jnp.concatenate(
        [jnp.stack(sums), in_bias_grad.reshape(model_width, -1).T], axis=0
    )
    small_grad = jnp.pad(small_grad, ((0, 128 - small_grad.shape[0]), (0, 0))).T
    down_shard = scatter_end(down)
    in_shard = scatter_end(inward)
    out_shard = scatter_end(outward)
    half = qkv_weight_grad.shape[1] // 2
    qkv_shard = jnp.concatenate(
        [
            scatter_end(scatter_start(qkv_weight_grad[:, :half], True)),
            scatter_end(scatter_start(qkv_weight_grad[:, half:], False)),
        ],
        axis=1,
    )
    small_shard = scatter_end(scatter_start(small_grad, True))
    columns = [small_shard[:, i] for i in range(len(vectors))]
    (
        bquery_shard,
        bvalue_shard,
        out_bias_shard,
        gain_one_shard,
        shift_one_shard,
        down_bias_shard,
        gain_two_shard,
        shift_two_shard,
    ) = columns
    in_bias_shard = small_shard[:, len(vectors) : len(vectors) + b_in.shape[0] // rows].reshape(-1)
    return (
        mixed,
        input_grad,
        qkv_shard,
        bquery_shard,
        bvalue_shard,
        out_shard,
        out_bias_shard,
        gain_one_shard,
        shift_one_shard,
        in_shard,
        in_bias_shard,
        down_shard,
        down_bias_shard,
        gain_two_shard,
        shift_two_shard,
    )


def solution(mesh):
    in_specs = (
        P(("dp", "seq"), None, None),
        P(("dp", "seq"), None),
        P(("dp", "seq"), None, None),
        P(("dp", "seq"), None),
        P(("dp", "seq")),
        P(("dp", "seq")),
        P(("dp", "seq"), None),
        P(("dp", "seq")),
        P(("dp", "seq")),
        P(("dp", "seq")),
        P(("dp", "seq"), None),
        P(("dp", "seq")),
        P(("dp", "seq"), None),
        P(("dp", "seq")),
        P(("dp", "seq")),
        P(("dp", "seq")),
    )
    out_specs = (
        P(("dp", "seq"), None, None),
        P(("dp", "seq"), None, None),
        P(("dp", "seq"), None),
        P(("dp", "seq")),
        P(("dp", "seq")),
        P(("dp", "seq"), None),
        P(("dp", "seq")),
        P(("dp", "seq")),
        P(("dp", "seq")),
        P(("dp", "seq"), None),
        P(("dp", "seq")),
        P(("dp", "seq"), None),
        P(("dp", "seq")),
        P(("dp", "seq")),
        P(("dp", "seq")),
    )
    return jax.shard_map(shards, mesh=mesh, in_specs=in_specs, out_specs=out_specs, check_vma=False)
```
